32 devices in a mesh: ax: 8 (over z, y), az: 2 (over x), rad: 2 (over core).
Axes of the slice: x: 2, y: 2, z: 4, core: 2. Of those that a mesh axis runs over, the one named last changes fastest.
Arguments:
- state: float32 [5, 64, 128, 1024], P(None, 'ax', 'rad', 'az'), may hold values from -6 to 6
- section: float32 [5, 64, 128, 1024], P(None, 'ax', 'rad', 'az'), may hold values from -6 to 6
- mean_axial: float32 [128], P('rad'), may hold values from 0.3 to 0.6
- mean_swirl: float32 [128], P('rad'), may hold values from 0.1 to 0.4
- mean_density: float32 [128], P('rad'), may hold values from 0.8 to 1.25
- sound_squared: float32 [128], P('rad'), may hold values from 0.8 to 1.25
Outputs:
- new_state: float32 [5, 64, 128, 1024], P(None, 'ax', 'rad', 'az')
- new_section: float32 [5, 64, 128, 1024], P(None, 'ax', 'rad', 'az')
The draws below stay inside these ranges and needn't reach their ends.
All inputs are finite; a program needn't handle non-finite values.
Results may differ from the reference program's by a relative error of at most 0.00005.
Values sent between devices are 32-bit elements; how exact they have to be, the bound alone decides.
A program may use at most 128 MiB of HBM per device.

```python
import math
import jax
import jax.numpy as jnp

NT = 1024
NX = 64
NR = 128


def draw_state(key, part):
    first_key = jax.random.fold_in(jax.random.fold_in(key, 11), 0)
    return jnp.clip(jax.random.normal(first_key, (5, NX, NR, NT), jnp.float32), -6.0, 6.0)


def steps_of(own_key, dims, cuts, smallest, largest):
    level, own = 1.0, jax.random.fold_in(own_key, 6)
    for dim, shards_of in cuts:
        steps = jnp.exp(jax.random.uniform(jax.random.fold_in(own, dim), (shards_of,), jnp.float32, smallest / len(cuts), largest / len(cuts)))
        level = level * jnp.repeat(steps, dims[dim] // shards_of).reshape([-1 if axis == dim else 1 for axis in range(len(dims))])
    return level


def scatter_about(rng, extent, scale, limit, cuts=(), kind=jnp.bfloat16):
    loudness = steps_of(rng, extent, cuts, -0.22, 0.18) if cuts else 1.0
    values = jax.random.normal(rng, extent, jnp.float32) * scale * loudness
    return jnp.minimum(jnp.maximum(values, -limit), limit).astype(kind)


def setup_inputs(seed: int = 0) -> dict:
    streams_of = jax.random.split(jax.random.key(seed), 7)
    return {
        "state": draw_state(jax.random.fold_in(streams_of[6], 71), 0),
        "section": scatter_about(streams_of[1], (5, NX, NR, NT), 1.0, 6.0, ((1, 8), (2, 2), (3, 2)), jnp.float32),
        "mean_axial": jnp.clip(0.3 + 0.3 * jax.random.uniform(streams_of[2], (NR,), jnp.float32) ** steps_of(streams_of[2], (NR,), ((0, 2),), -0.2, 0.2), 0.3, 0.6),
        "mean_swirl": jnp.clip(0.1 + 0.3 * jax.random.uniform(streams_of[3], (NR,), jnp.float32) ** steps_of(streams_of[3], (NR,), ((0, 2),), -0.2, 0.2), 0.1, 0.4),
        "mean_density": jnp.clip(0.8 + 0.45 * jax.random.uniform(streams_of[4], (NR,), jnp.float32) ** steps_of(streams_of[4], (NR,), ((0, 2),), -0.2, 0.2), 0.8, 1.25),
        "sound_squared": jnp.clip(0.8 + 0.45 * jax.random.uniform(streams_of[5], (NR,), jnp.float32) ** steps_of(streams_of[5], (NR,), ((0, 2),), -0.2, 0.2), 0.8, 1.25),
    }


drp_coeffs = (0.770882380518, -0.166705904415, 0.020843142770)
section_keep = -0.4178904745
section_gain = 0.3792103129999
time_step = 0.25


def axial_derivative(fields):
    count = fields.shape[1]
    padded = jnp.pad(fields, ((0, 0), (3, 3), (0, 0), (0, 0)))
    result = jnp.zeros_like(fields)
    for offset in range(1, 4):
        upper = padded[:, 3 + offset:3 + offset + count]
        lower = padded[:, 3 - offset:3 - offset + count]
        result = result + drp_coeffs[offset - 1] * (upper - lower)
    return result


def radial_derivative(pair):
    count = pair.shape[2]
    signs = jnp.array([-1.0, 1.0], dtype=jnp.float32).reshape(2, 1, 1, 1)
    lower_wall = signs * jnp.flip(pair[:, :, 0:3], axis=2)
    upper_wall = signs * jnp.flip(pair[:, :, count - 3:count], axis=2)
    padded = jnp.concatenate([lower_wall, pair, upper_wall], axis=2)
    result = jnp.zeros_like(pair)
    for offset in range(1, 4):
        upper = padded[:, :, 3 + offset:3 + offset + count]
        lower = padded[:, :, 3 - offset:3 - offset + count]
        result = result + drp_coeffs[offset - 1] * (upper - lower)
    return result


def azimuthal_derivative(fields):
    spectrum = jnp.fft.rfft(fields, axis=-1)
    modes = jnp.arange(NT // 2 + 1)
    factor = jnp.where(modes == NT // 2, 0, modes).astype(jnp.float32)
    return jnp.fft.irfft(1j * factor * spectrum, n=NT, axis=-1).astype(jnp.float32)


def reference(state, section, mean_axial, mean_swirl, mean_density, sound_squared):
    radius = NT / (2.0 * math.pi) + jnp.arange(NR).astype(jnp.float32) + 0.5
    inv_radius = (1.0 / radius)[:, None]
    axial_speed = mean_axial[:, None]
    swirl_rate = mean_swirl[:, None] * inv_radius
    density = mean_density[:, None]
    inv_density = 1.0 / density
    stiffness = density * sound_squared[:, None]
    axial_grad = axial_derivative(state)
    azim_grad = azimuthal_derivative(state)
    radial_grad = radial_derivative(state[2::2])
    convect = axial_speed * axial_grad + swirl_rate * azim_grad
    diverge = axial_grad[1] + radial_grad[0] + inv_radius * azim_grad[3]
    rhs = jnp.stack([
        -(convect[0] + density * diverge),
        -(convect[1] + axial_grad[4] * inv_density),
        -(convect[2] + radial_grad[1] * inv_density),
        -(convect[3] + inv_radius * azim_grad[4] * inv_density),
        -(convect[4] + stiffness * diverge),
    ])
    new_section = section_keep * section + time_step * rhs
    return state + section_gain * new_section, new_section
```

```python
import functools
import math

import jax
import jax.numpy as jnp
import numpy as np
from jax import lax
from jax.experimental import pallas as pl
from jax.experimental.pallas import tpu as pltpu
from jax.sharding import PartitionSpec as P

NT = 1024
MESH = pl.DeviceIdType.MESH

drp_coeffs = (0.770882380518, -0.166705904415, 0.02084314277)
section_keep = -0.4178904745
section_gain = 0.3792103129999
time_step = 0.25
HALO = 3
RIM = 8
CUTS = 4
NODES = 64
WIDTH = 2 * NODES


def split(full):
    full = full.astype(np.float32)
    high = full.astype(jnp.bfloat16)
    low = (full - high.astype(np.float32)).astype(jnp.bfloat16)
    return np.stack([high, low])


def near_table(local):
    s = np.arange(local)[:, None]
    t = np.arange(local)[None, :]
    spacing = t - s
    angle = np.pi * spacing / NT
    safe = np.where(spacing == 0, 1.0, np.sin(angle))
    parity = 1.0 - 2.0 * (spacing % 2)
    return split(np.where(spacing == 0, 0.0, 0.5 * parity * np.cos(angle) / safe))


def quadrature():
    step = 0.16
    u = (np.arange(NODES) + 0.5) * step
    scale = 2.0 * np.pi / NT
    t = scale * np.sinh(u)
    weight = step * scale * np.cosh(u) * (NT / np.pi) / -np.expm1(-NT * t)
    return t, weight


def far_tables(owners, local):
    t, weight = quadrature()
    k = np.arange(local)[:, None]
    sign = 1.0 - 2.0 * (k % 2)
    into = np.concatenate([sign * np.exp(-k * t), sign * np.exp(-(local - 1 - k) * t)], axis=1)
    t, weight = t[:, None], weight[:, None]
    j = np.arange(local)[None, :]
    sign = 1.0 - 2.0 * (j % 2)
    outof = []
    for d in range(1, owners):
        below = -0.5 * sign * weight * np.exp(-(NT - d * local - j) * t)
        above = 0.5 * sign * weight * np.exp(-(d * local + j - local + 1) * t)
        outof.append(split(np.concatenate([below, above], axis=0)))
    return split(into), np.stack(outof)


def product(values, high_table, low_table):
    high = values.astype(jnp.bfloat16)
    low = (values - high.astype(jnp.float32)).astype(jnp.bfloat16)
    dot = functools.partial(jnp.dot, preferred_element_type=jnp.float32)
    return dot(high, high_table) + dot(low, high_table) + dot(high, low_table)


def kernel(
    sizes, state, section, axial_speed, swirl, density_in, sound, near_in, into_in, outof_in, ns, nst,
    st, pr, halo, relay, sums, other, near, into, outof, coef, means,
    load_sem, az_send, az_recv, ax_send, ax_recv, hop_send, hop_recv, pass_send, rad_send, rad_recv,
):
    n_ax, n_az, n_rad, count, rows, local = sizes
    cut = rows // CUTS
    ax = lax.axis_index("ax")
    az = lax.axis_index("az")
    rad = lax.axis_index("rad")
    has_prev, has_next = ax > 0, ax < n_ax - 1
    has_low, has_high = rad > 0, rad < n_rad - 1

    levels = n_ax // 2 if n_ax % 2 == 0 and n_ax <= 2 * CUTS else 0
    level = lax.div(ax, 2)
    odd = lax.rem(ax, 2) == 1
    even = jnp.logical_not(odd)
    zero = jnp.int32(0)
    if levels:
        rest = lax.div((levels - 1 - level) * CUTS, levels)
        gone = lax.div(level * CUTS, levels)
        hop_up = jnp.where(jnp.logical_and(odd, has_next), rest, zero)
        hop_down = jnp.where(jnp.logical_and(even, has_prev), gone, zero)
        pass_up = jnp.where(jnp.logical_and(even, ax + 2 < n_ax), rest, zero)
        pass_down = jnp.where(jnp.logical_and(odd, ax >= 3), gone, zero)
    else:
        hop_up = hop_down = pass_up = pass_down = zero
    hops = range(CUTS - 1 if levels else 0)

    def az_copy(d, c):
        return pltpu.make_async_remote_copy(
            src_ref=sums.at[:, c],
            dst_ref=other.at[d - 1, :, c],
            send_sem=az_send.at[d - 1, c],
            recv_sem=az_recv.at[d - 1, c],
            device_id={"az": lax.rem(az + d, n_az)},
            device_id_type=MESH,
        )

    def edge(up, q):
        return state.at[:, pl.ds(count - HALO if up else 0, HALO), pl.ds(q * cut, cut)]

    def landing(up, q):
        return halo.at[0 if up else 1, :, :, pl.ds(q * cut, cut)]

    def ax_copy(up, q):
        way = 0 if up else 1
        return pltpu.make_async_remote_copy(
            src_ref=edge(up, q),
            dst_ref=landing(up, q),
            send_sem=ax_send.at[way, q],
            recv_sem=ax_recv.at[way, q],
            device_id={"ax": ax + 1 if up else ax - 1},
            device_id_type=MESH,
        )

    def hop_copy(up, q):
        return pltpu.make_async_remote_copy(
            src_ref=edge(up, q),
            dst_ref=relay.at[q],
            send_sem=hop_send.at[q],
            recv_sem=hop_recv.at[q],
            device_id={"ax": ax - 1 if up else ax + 1},
            device_id_type=MESH,
        )

    def pass_copy(up, q):
        return pltpu.make_async_remote_copy(
            src_ref=relay.at[q],
            dst_ref=landing(up, q),
            send_sem=pass_send.at[q],
            recv_sem=ax_recv.at[0 if up else 1, q],
            device_id={"ax": ax + 2 if up else ax - 2},
            device_id_type=MESH,
        )

    def rad_copy(up, k):
        return pltpu.make_async_remote_copy(
            src_ref=state.at[2 + 2 * k, :, pl.ds(rows - RIM if up else 0, RIM)],
            dst_ref=pr.at[k, :, pl.ds(0 if up else rows + RIM, RIM)],
            send_sem=rad_send.at[0 if up else 1, k],
            recv_sem=rad_recv.at[0 if up else 1, k],
            device_id={"rad": rad + 1 if up else rad - 1},
            device_id_type=MESH,
        )

    loads = [
        pltpu.make_async_copy(state, st.at[:, pl.ds(HALO, count)], load_sem.at[0]),
        pltpu.make_async_copy(into_in, into, load_sem.at[1]),
        pltpu.make_async_copy(section, ns, load_sem.at[2]),
        pltpu.make_async_copy(state.at[2], pr.at[0, :, pl.ds(RIM, rows)], load_sem.at[3]),
        pltpu.make_async_copy(state.at[4], pr.at[1, :, pl.ds(RIM, rows)], load_sem.at[4]),
        pltpu.make_async_copy(near_in, near, load_sem.at[5]),
        pltpu.make_async_copy(outof_in, outof, load_sem.at[6]),
    ]
    vectors = [
        pltpu.make_async_copy(ref, means.at[i], load_sem.at[7 + i])
        for i, ref in enumerate((axial_speed, swirl, density_in, sound))
    ]

    barrier = pltpu.get_barrier_semaphore()

    def greet(axis, index):
        pl.semaphore_signal(barrier, inc=1, device_id={axis: index}, device_id_type=MESH)

    met = zero + (n_az - 1)
    for d in (-2, -1, 1, 2) if levels else (-1, 1):
        there = jnp.logical_and(ax + d >= 0, ax + d < n_ax)
        pl.when(there)(lambda: greet("ax", ax + d))
        met = met + there.astype(jnp.int32)
    for d in range(1, n_az):
        greet("az", lax.rem(az + d, n_az))
    pl.when(has_low)(lambda: greet("rad", rad - 1))
    pl.when(has_high)(lambda: greet("rad", rad + 1))
    met = met + has_low.astype(jnp.int32) + has_high.astype(jnp.int32)
    for copy in vectors + loads:
        copy.start()
    pl.semaphore_wait(barrier, met)

    up_direct = lambda q: jnp.logical_and(has_next, q >= hop_up)
    down_direct = lambda q: jnp.logical_and(has_prev, q >= hop_down)

    def send(q, first):
        up = jnp.logical_and(up_direct(q), odd if first else even)
        down = jnp.logical_and(down_direct(q), even if first else odd)
        pl.when(up)(lambda: ax_copy(True, q).start())
        pl.when(down)(lambda: ax_copy(False, q).start())

    for q in hops:
        pl.when(q < hop_up)(lambda: hop_copy(True, q).start())
        pl.when(q < hop_down)(lambda: hop_copy(False, q).start())
    for first in (True, False):
        for q in range(CUTS):
            send(q, first)
    for k in range(2):
        pl.when(has_high)(lambda: rad_copy(True, k).start())
        pl.when(has_low)(lambda: rad_copy(False, k).start())

    for copy in vectors:
        copy.wait()

    pick = lax.broadcasted_iota(jnp.int32, (rows, rows), 0) == lax.broadcasted_iota(
        jnp.int32, (rows, rows), 1
    )

    def column(i):
        line = jnp.broadcast_to(means[i], (rows, rows))
        return jnp.sum(jnp.where(pick, line, 0.0), axis=1, keepdims=True)

    cell = lax.broadcasted_iota(jnp.int32, (rows, local), 0) + rad * rows
    inv_radius = 1.0 / (NT / (2.0 * math.pi) + cell.astype(jnp.float32) + 0.5)
    density = jnp.broadcast_to(column(2), (rows, local))
    minus = -time_step
    inverse = minus / density
    stiff = minus * density * column(3)
    coef[0] = jnp.broadcast_to(minus * column(0), (rows, local))
    coef[1] = minus * column(1) * inv_radius
    coef[2] = minus * density
    coef[3] = stiff
    coef[4] = inverse
    coef[5] = minus * density * inv_radius
    coef[6] = stiff * inv_radius
    coef[7] = inverse * inv_radius

    for copy in loads[:2]:
        copy.wait()

    def gather(c, carry):
        flat = st[:, HALO + c].reshape(5 * rows, local)
        sums[:, c] = product(flat, into[0], into[1]).reshape(5, rows, WIDTH)
        for d in range(1, n_az):
            az_copy(d, c).start()
        return carry

    lax.fori_loop(0, count, gather, 0)

    for start in (0, count + HALO):
        st[:, pl.ds(start, HALO)] = jnp.zeros((5, HALO, rows, local), jnp.float32)

    for copy in loads[2:]:
        copy.wait()

    def wall(low):
        def fill(c, carry):
            for k, sign in enumerate((-1.0, 1.0)):
                for j in range(3):
                    if low:
                        pr[k, c, pl.ds(RIM - 1 - j, 1)] = sign * pr[k, c, pl.ds(RIM + j, 1)]
                    else:
                        pr[k, c, pl.ds(RIM + rows + j, 1)] = sign * pr[
                            k, c, pl.ds(RIM + rows - 1 - j, 1)
                        ]
            return carry

        lax.fori_loop(0, count, fill, 0)

    pl.when(jnp.logical_not(has_low))(lambda: wall(True))
    pl.when(jnp.logical_not(has_high))(lambda: wall(False))
    for k in range(2):
        pl.when(has_low)(lambda: rad_copy(True, k).wait_recv())
        pl.when(has_high)(lambda: rad_copy(False, k).wait_recv())

    def radial(k, c):
        total = jnp.zeros((rows, local), jnp.float32)
        for j in range(1, 4):
            total += drp_coeffs[j - 1] * (
                pr[k, c, pl.ds(RIM + j, rows)] - pr[k, c, pl.ds(RIM - j, rows)]
            )
        return total

    def axial(f, c):
        total = jnp.zeros((rows, local), jnp.float32)
        for j in range(1, 4):
            total += drp_coeffs[j - 1] * (st[f, c + HALO + j] - st[f, c + HALO - j])
        return total

    def pass_on(q):
        @pl.when(q < pass_up)
        def _():
            hop_copy(True, q).wait_recv()
            pass_copy(True, q).start()

        @pl.when(q < pass_down)
        def _():
            hop_copy(False, q).wait_recv()
            pass_copy(False, q).start()

    def plane(c, carry):
        spread = radial(0, c)
        along = axial(1, c)
        press = axial(4, c)
        speed = coef[0]
        ns[0, c] = section_keep * ns[0, c] + speed * axial(0, c) + coef[2] * (along + spread)
        ns[1, c] = section_keep * ns[1, c] + speed * along + coef[4] * press
        ns[2, c] = section_keep * ns[2, c] + speed * axial(2, c) + coef[4] * radial(1, c)
        ns[3, c] = section_keep * ns[3, c] + speed * axial(3, c)
        ns[4, c] = section_keep * ns[4, c] + speed * press + coef[3] * (along + spread)
        g = product(st[:, HALO + c].reshape(5 * rows, local), near[0], near[1])
        for d in range(1, n_az):
            az_copy(d, c).wait_recv()
            g += product(other[d - 1, :, c].reshape(5 * rows, WIDTH), outof[d - 1, 0], outof[d - 1, 1])
        g = g.reshape(5, rows, local)
        rate = coef[1]
        ns[0, c] += rate * g[0] + coef[5] * g[3]
        ns[1, c] += rate * g[1]
        ns[2, c] += rate * g[2]
        ns[3, c] += rate * g[3] + coef[7] * g[4]
        ns[4, c] += rate * g[4] + coef[6] * g[3]
        for f in range(5):
            nst[f, c] = st[f, HALO + c] + section_gain * ns[f, c]
        for q in hops:
            pl.when(c == min(2 * q + 1, count - 1))(lambda: pass_on(q))
        return carry

    lax.fori_loop(0, count, plane, 0)

    def rim(up, q):
        way = 0 if up else 1
        lines = pl.ds(q * cut, cut)
        speed, dense, stiff, inverse = coef[0, lines], coef[2, lines], coef[3, lines], coef[4, lines]
        for reach in range(HALO):
            p = reach if up else count - 1 - reach
            grads = []
            for f in range(5):
                total = jnp.zeros((cut, local), jnp.float32)
                for j in range(reach + 1, HALO + 1):
                    past = j - reach - 1
                    total += drp_coeffs[j - 1] * halo[way, f, HALO - 1 - past if up else past, lines]
                grads.append(-total if up else total)
            more = (
                speed * grads[0] + dense * grads[1],
                speed * grads[1] + inverse * grads[4],
                speed * grads[2],
                speed * grads[3],
                speed * grads[4] + stiff * grads[1],
            )
            for f in range(5):
                value = ns[f, p, lines] + more[f]
                ns[f, p, lines] = value
                nst[f, p, lines] = st[f, HALO + p, lines] + section_gain * value

    for q in range(CUTS):
        @pl.when(has_prev)
        def _():
            ax_copy(True, q).wait_recv()
            rim(True, q)

        @pl.when(has_next)
        def _():
            ax_copy(False, q).wait_recv()
            rim(False, q)

    def drain(c, carry):
        for d in range(1, n_az):
            az_copy(d, c).wait_send()
        return carry

    lax.fori_loop(0, count, drain, 0)
    for q in range(CUTS):
        pl.when(up_direct(q))(lambda: ax_copy(True, q).wait_send())
        pl.when(down_direct(q))(lambda: ax_copy(False, q).wait_send())
    for q in hops:
        pl.when(q < hop_up)(lambda: hop_copy(True, q).wait_send())
        pl.when(q < hop_down)(lambda: hop_copy(False, q).wait_send())
        pl.when(q < pass_up)(lambda: pass_copy(True, q).wait_send())
        pl.when(q < pass_down)(lambda: pass_copy(False, q).wait_send())
    for k in range(2):
        pl.when(has_high)(lambda: rad_copy(True, k).wait_send())
        pl.when(has_low)(lambda: rad_copy(False, k).wait_send())


def write_kernel(ns, nst, out_state, out_section, sem):
    copies = []
    for c in range(ns.shape[1]):
        copies.append(pltpu.make_async_copy(ns.at[:, c], out_section.at[:, c], sem.at[0, c]))
        copies.append(pltpu.make_async_copy(nst.at[:, c], out_state.at[:, c], sem.at[1, c]))
    for copy in copies:
        copy.start()
    for copy in copies:
        copy.wait()


def body(mesh_sizes, state, section, mean_axial, mean_swirl, mean_density, sound_squared):
    n_ax, n_az, n_rad = mesh_sizes
    _, count, rows, local = state.shape
    near_t = jnp.asarray(near_table(local))
    into_t, outof_t = (jnp.asarray(table) for table in far_tables(n_az, local))
    whole = (5, count, rows, local)
    far = pl.BlockSpec(memory_space=pltpu.HBM)
    near = pl.BlockSpec(memory_space=pltpu.VMEM)
    f32 = jnp.float32
    dma = pltpu.SemaphoreType.DMA
    pin = functools.partial(pltpu.with_memory_space_constraint, memory_space=pltpu.HBM)
    cut = rows // CUTS
    ns, nst = pl.pallas_call(
        functools.partial(kernel, (n_ax, n_az, n_rad, count, rows, local)),
        out_shape=tuple(pltpu.VMEM(shape, f32) for shape in (whole, whole)),
        in_specs=[far] * 9,
        out_specs=(near,) * 2,
        scratch_shapes=[
            pltpu.VMEM((5, count + 2 * HALO, rows, local), f32),
            pltpu.VMEM((2, count, rows + 2 * RIM, local), f32),
            pltpu.VMEM((2, 5, HALO, rows, local), f32),
            pltpu.VMEM((CUTS - 1, 5, HALO, cut, local), f32),
            pltpu.VMEM((5, count, rows, WIDTH), f32),
            pltpu.VMEM((n_az - 1, 5, count, rows, WIDTH), f32),
            pltpu.VMEM((2, local, local), jnp.bfloat16),
            pltpu.VMEM((2, local, WIDTH), jnp.bfloat16),
            pltpu.VMEM((n_az - 1, 2, WIDTH, local), jnp.bfloat16),
            pltpu.VMEM((8, rows, local), f32),
            pltpu.VMEM((4, 1, rows), f32),
            dma((11,)),
            dma((n_az - 1, count)),
            dma((n_az - 1, count)),
            dma((2, CUTS)),
            dma((2, CUTS)),
            dma((CUTS - 1,)),
            dma((CUTS - 1,)),
            dma((CUTS - 1,)),
            dma((2, 2)),
            dma((2, 2)),
        ],
        compiler_params=pltpu.CompilerParams(
            collective_id=0, has_side_effects=True, vmem_limit_bytes=36 * 2**20
        ),
        cost_estimate=pl.CostEstimate(
            flops=6 * 5 * count * rows * local * NT,
            bytes_accessed=4 * 4 * 5 * count * rows * local,
            transcendentals=0,
        ),
    )(
        pin(state),
        pin(section),
        pin(mean_axial[None]),
        pin(mean_swirl[None]),
        pin(mean_density[None]),
        pin(sound_squared[None]),
        pin(near_t),
        pin(into_t),
        pin(outof_t),
    )
    return pl.pallas_call(
        write_kernel,
        out_shape=(jax.ShapeDtypeStruct(whole, f32), jax.ShapeDtypeStruct(whole, f32)),
        in_specs=[near] * 2,
        out_specs=(far, far),
        scratch_shapes=[dma((2, count))],
        compiler_params=pltpu.CompilerParams(vmem_limit_bytes=4 * 2**20),
    )(ns, nst)


def solution(mesh):
    spec = P(None, "ax", "rad", "az")
    sizes = (mesh.shape["ax"], mesh.shape["az"], mesh.shape["rad"])
    return jax.shard_map(
        functools.partial(body, sizes),
        mesh=mesh,
        in_specs=(spec, spec, P("rad"), P("rad"), P("rad"), P("rad")),
        out_specs=(spec, spec),
        check_vma=False,
    )
```

```python
import functools
import math

import jax
import jax.numpy as jnp
import numpy as np
from jax import lax
from jax.experimental import pallas as pl
from jax.experimental.pallas import tpu as pltpu
from jax.sharding import PartitionSpec as P

NT = 1024
MESH = pl.DeviceIdType.MESH

drp_coeffs = (0.770882380518, -0.166705904415, 0.02084314277)
section_keep = -0.4178904745
section_gain = 0.3792103129999
time_step = 0.25
HALO = 3
RIM = 8
CUTS = 4
NODES = 64
WIDTH = 2 * NODES


def split(full):
    full = full.astype(np.float32)
    high = full.astype(jnp.bfloat16)
    low = (full - high.astype(np.float32)).astype(jnp.bfloat16)
    return np.stack([high, low])


def near_table(local):
    s = np.arange(local)[:, None]
    t = np.arange(local)[None, :]
    spacing = t - s
    angle = np.pi * spacing / NT
    safe = np.where(spacing == 0, 1.0, np.sin(angle))
    parity = 1.0 - 2.0 * (spacing % 2)
    return split(np.where(spacing == 0, 0.0, 0.5 * parity * np.cos(angle) / safe))


def quadrature():
    step = 0.16
    u = (np.arange(NODES) + 0.5) * step
    scale = 2.0 * np.pi / NT
    t = scale * np.sinh(u)
    weight = step * scale * np.cosh(u) * (NT / np.pi) / -np.expm1(-NT * t)
    return t, weight


def far_tables(owners, local):
    t, weight = quadrature()
    k = np.arange(local)[:, None]
    sign = 1.0 - 2.0 * (k % 2)
    into = np.concatenate([sign * np.exp(-k * t), sign * np.exp(-(local - 1 - k) * t)], axis=1)
    t, weight = t[:, None], weight[:, None]
    j = np.arange(local)[None, :]
    sign = 1.0 - 2.0 * (j % 2)
    outof = []
    for d in range(1, owners):
        below = -0.5 * sign * weight * np.exp(-(NT - d * local - j) * t)
        above = 0.5 * sign * weight * np.exp(-(d * local + j - local + 1) * t)
        outof.append(split(np.concatenate([below, above], axis=0)))
    return split(into), np.stack(outof)


def product(values, high_table, low_table):
    high = values.astype(jnp.bfloat16)
    low = (values - high.astype(jnp.float32)).astype(jnp.bfloat16)
    dot = functools.partial(jnp.dot, preferred_element_type=jnp.float32)
    return dot(high, high_table) + dot(low, high_table) + dot(high, low_table)


def rim_terms(halo, way, lines, coef, rows, reach):
    grads = []
    for f in range(5):
        total = 0.0
        for j in range(reach + 1, HALO + 1):
            past = j - reach - 1
            total += drp_coeffs[j - 1] * halo[way, f, past if way else HALO - 1 - past, lines]
        grads.append(total if way else -total)
    speed, dense, stiff, inverse = coef[0, rows], coef[2, rows], coef[3, rows], coef[4, rows]
    return (
        speed * grads[0] + dense * grads[1],
        speed * grads[1] + inverse * grads[4],
        speed * grads[2],
        speed * grads[3],
        speed * grads[4] + stiff * grads[1],
    )


def kernel(
    sizes, state, section, axial_speed, swirl, density_in, sound, near_in, into_in, outof_in, ns, nst, late, coef,
    st, pr, halo, relay, sums, other, near, into, outof, means,
    load_sem, az_send, az_recv, ax_send, ax_recv, hop_send, hop_recv, pass_send, rad_send, rad_recv,
):
    n_ax, n_az, n_rad, count, rows, local = sizes
    cut = rows // CUTS
    ax = lax.axis_index("ax")
    az = lax.axis_index("az")
    rad = lax.axis_index("rad")
    has_prev, has_next = ax > 0, ax < n_ax - 1
    has_low, has_high = rad > 0, rad < n_rad - 1

    levels = n_ax // 2 if n_ax % 2 == 0 and n_ax <= 2 * CUTS else 0
    level = lax.div(ax, 2)
    odd = lax.rem(ax, 2) == 1
    even = jnp.logical_not(odd)
    zero = jnp.int32(0)
    if levels:
        rest = lax.div((levels - 1 - level) * CUTS, levels)
        gone = lax.div(level * CUTS, levels)
        hop_up = jnp.where(jnp.logical_and(odd, has_next), rest, zero)
        hop_down = jnp.where(jnp.logical_and(even, has_prev), gone, zero)
        pass_up = jnp.where(jnp.logical_and(even, ax + 2 < n_ax), rest, zero)
        pass_down = jnp.where(jnp.logical_and(odd, ax >= 3), gone, zero)
    else:
        hop_up = hop_down = pass_up = pass_down = zero
    hops = range(CUTS - 1 if levels else 0)

    def az_copy(d, c):
        return pltpu.make_async_remote_copy(
            src_ref=sums.at[:, c],
            dst_ref=other.at[d - 1, :, c],
            send_sem=az_send.at[d - 1, c],
            recv_sem=az_recv.at[d - 1, c],
            device_id={"az": lax.rem(az + d, n_az)},
            device_id_type=MESH,
        )

    def edge(up, q):
        return state.at[:, pl.ds(count - HALO if up else 0, HALO), pl.ds(q * cut, cut)]

    def landing(up, q):
        way = 0 if up else 1
        return late.at[way] if q == CUTS - 1 else halo.at[way, :, :, pl.ds(q * cut, cut)]

    def ax_copy(up, q):
        way = 0 if up else 1
        return pltpu.make_async_remote_copy(
            src_ref=edge(up, q),
            dst_ref=landing(up, q),
            send_sem=ax_send.at[way, q],
            recv_sem=ax_recv.at[way, q],
            device_id={"ax": ax + 1 if up else ax - 1},
            device_id_type=MESH,
        )

    def hop_copy(up, q):
        return pltpu.make_async_remote_copy(
            src_ref=edge(up, q),
            dst_ref=relay.at[q],
            send_sem=hop_send.at[q],
            recv_sem=hop_recv.at[q],
            device_id={"ax": ax - 1 if up else ax + 1},
            device_id_type=MESH,
        )

    def pass_copy(up, q):
        return pltpu.make_async_remote_copy(
            src_ref=relay.at[q],
            dst_ref=landing(up, q),
            send_sem=pass_send.at[q],
            recv_sem=ax_recv.at[0 if up else 1, q],
            device_id={"ax": ax + 2 if up else ax - 2},
            device_id_type=MESH,
        )

    def rad_copy(up, k):
        return pltpu.make_async_remote_copy(
            src_ref=state.at[2 + 2 * k, :, pl.ds(rows - RIM if up else 0, RIM)],
            dst_ref=pr.at[k, :, pl.ds(0 if up else rows + RIM, RIM)],
            send_sem=rad_send.at[0 if up else 1, k],
            recv_sem=rad_recv.at[0 if up else 1, k],
            device_id={"rad": rad + 1 if up else rad - 1},
            device_id_type=MESH,
        )

    loads = [
        pltpu.make_async_copy(state, st.at[:, pl.ds(HALO, count)], load_sem.at[0]),
        pltpu.make_async_copy(into_in, into, load_sem.at[1]),
        pltpu.make_async_copy(section, ns, load_sem.at[2]),
        pltpu.make_async_copy(state.at[2], pr.at[0, :, pl.ds(RIM, rows)], load_sem.at[3]),
        pltpu.make_async_copy(state.at[4], pr.at[1, :, pl.ds(RIM, rows)], load_sem.at[4]),
        pltpu.make_async_copy(near_in, near, load_sem.at[5]),
        pltpu.make_async_copy(outof_in, outof, load_sem.at[6]),
    ]
    vectors = [
        pltpu.make_async_copy(ref, means.at[i], load_sem.at[7 + i])
        for i, ref in enumerate((axial_speed, swirl, density_in, sound))
    ]

    barrier = pltpu.get_barrier_semaphore()

    def greet(axis, index):
        pl.semaphore_signal(barrier, inc=1, device_id={axis: index}, device_id_type=MESH)

    met = zero + (n_az - 1)
    for d in (-2, -1, 1, 2) if levels else (-1, 1):
        there = jnp.logical_and(ax + d >= 0, ax + d < n_ax)
        pl.when(there)(lambda: greet("ax", ax + d))
        met = met + there.astype(jnp.int32)
    for d in range(1, n_az):
        greet("az", lax.rem(az + d, n_az))
    pl.when(has_low)(lambda: greet("rad", rad - 1))
    pl.when(has_high)(lambda: greet("rad", rad + 1))
    met = met + has_low.astype(jnp.int32) + has_high.astype(jnp.int32)
    pl.semaphore_wait(barrier, met)

    up_direct = lambda q: jnp.logical_and(has_next, q >= hop_up)
    down_direct = lambda q: jnp.logical_and(has_prev, q >= hop_down)

    def send(q, first):
        up = jnp.logical_and(up_direct(q), odd if first else even)
        down = jnp.logical_and(down_direct(q), even if first else odd)
        pl.when(up)(lambda: ax_copy(True, q).start())
        pl.when(down)(lambda: ax_copy(False, q).start())

    for q in hops:
        pl.when(q < hop_up)(lambda: hop_copy(True, q).start())
        pl.when(q < hop_down)(lambda: hop_copy(False, q).start())
    for first in (True, False):
        for q in range(CUTS):
            send(q, first)
    for k in range(2):
        pl.when(has_high)(lambda: rad_copy(True, k).start())
        pl.when(has_low)(lambda: rad_copy(False, k).start())

    for copy in vectors + loads:
        copy.start()
    for copy in vectors:
        copy.wait()

    pick = lax.broadcasted_iota(jnp.int32, (rows, rows), 0) == lax.broadcasted_iota(
        jnp.int32, (rows, rows), 1
    )

    def column(i):
        line = jnp.broadcast_to(means[i], (rows, rows))
        return jnp.sum(jnp.where(pick, line, 0.0), axis=1, keepdims=True)

    cell = lax.broadcasted_iota(jnp.int32, (rows, local), 0) + rad * rows
    inv_radius = 1.0 / (NT / (2.0 * math.pi) + cell.astype(jnp.float32) + 0.5)
    density = jnp.broadcast_to(column(2), (rows, local))
    minus = -time_step
    inverse = minus / density
    stiff = minus * density * column(3)
    coef[0] = jnp.broadcast_to(minus * column(0), (rows, local))
    coef[1] = minus * column(1) * inv_radius
    coef[2] = minus * density
    coef[3] = stiff
    coef[4] = inverse
    coef[5] = minus * density * inv_radius
    coef[6] = stiff * inv_radius
    coef[7] = inverse * inv_radius

    for copy in loads[:2]:
        copy.wait()

    def gather(c, carry):
        flat = st[:, HALO + c].reshape(5 * rows, local)
        sums[:, c] = product(flat, into[0], into[1]).reshape(5, rows, WIDTH)
        for d in range(1, n_az):
            az_copy(d, c).start()
        return carry

    lax.fori_loop(0, count, gather, 0)

    for start in (0, count + HALO):
        st[:, pl.ds(start, HALO)] = jnp.zeros((5, HALO, rows, local), jnp.float32)

    for copy in loads[2:]:
        copy.wait()

    def wall(low):
        def fill(c, carry):
            for k, sign in enumerate((-1.0, 1.0)):
                for j in range(3):
                    if low:
                        pr[k, c, pl.ds(RIM - 1 - j, 1)] = sign * pr[k, c, pl.ds(RIM + j, 1)]
                    else:
                        pr[k, c, pl.ds(RIM + rows + j, 1)] = sign * pr[
                            k, c, pl.ds(RIM + rows - 1 - j, 1)
                        ]
            return carry

        lax.fori_loop(0, count, fill, 0)

    pl.when(jnp.logical_not(has_low))(lambda: wall(True))
    pl.when(jnp.logical_not(has_high))(lambda: wall(False))
    for k in range(2):
        pl.when(has_low)(lambda: rad_copy(True, k).wait_recv())
        pl.when(has_high)(lambda: rad_copy(False, k).wait_recv())

    def radial(k, c):
        total = jnp.zeros((rows, local), jnp.float32)
        for j in range(1, 4):
            total += drp_coeffs[j - 1] * (
                pr[k, c, pl.ds(RIM + j, rows)] - pr[k, c, pl.ds(RIM - j, rows)]
            )
        return total

    def axial(f, c):
        total = jnp.zeros((rows, local), jnp.float32)
        for j in range(1, 4):
            total += drp_coeffs[j - 1] * (st[f, c + HALO + j] - st[f, c + HALO - j])
        return total

    for way, there in enumerate((has_prev, has_next)):
        @pl.when(jnp.logical_not(there))
        def _():
            late[way] = jnp.zeros_like(late[way])

    def pass_on(q):
        @pl.when(q < pass_up)
        def _():
            hop_copy(True, q).wait_recv()
            pass_copy(True, q).start()

        @pl.when(q < pass_down)
        def _():
            hop_copy(False, q).wait_recv()
            pass_copy(False, q).start()

    def plane(c, carry):
        spread = radial(0, c)
        along = axial(1, c)
        press = axial(4, c)
        speed = coef[0]
        ns[0, c] = section_keep * ns[0, c] + speed * axial(0, c) + coef[2] * (along + spread)
        ns[1, c] = section_keep * ns[1, c] + speed * along + coef[4] * press
        ns[2, c] = section_keep * ns[2, c] + speed * axial(2, c) + coef[4] * radial(1, c)
        ns[3, c] = section_keep * ns[3, c] + speed * axial(3, c)
        ns[4, c] = section_keep * ns[4, c] + speed * press + coef[3] * (along + spread)
        g = product(st[:, HALO + c].reshape(5 * rows, local), near[0], near[1])
        for d in range(1, n_az):
            az_copy(d, c).wait_recv()
            g += product(other[d - 1, :, c].reshape(5 * rows, WIDTH), outof[d - 1, 0], outof[d - 1, 1])
        g = g.reshape(5, rows, local)
        rate = coef[1]
        ns[0, c] += rate * g[0] + coef[5] * g[3]
        ns[1, c] += rate * g[1]
        ns[2, c] += rate * g[2]
        ns[3, c] += rate * g[3] + coef[7] * g[4]
        ns[4, c] += rate * g[4] + coef[6] * g[3]
        for f in range(5):
            nst[f, c] = st[f, HALO + c] + section_gain * ns[f, c]
        for q in hops:
            pl.when(c == min(2 * q + 1, count - 1))(lambda: pass_on(q))
        return carry

    lax.fori_loop(0, count, plane, 0)

    def rim(up, q):
        lines = pl.ds(q * cut, cut)
        for reach in range(HALO):
            p = reach if up else count - 1 - reach
            more = rim_terms(halo, 0 if up else 1, lines, coef, lines, reach)
            for f in range(5):
                value = ns[f, p, lines] + more[f]
                ns[f, p, lines] = value
                nst[f, p, lines] = st[f, HALO + p, lines] + section_gain * value

    for q in range(CUTS - 1):
        @pl.when(has_prev)
        def _():
            ax_copy(True, q).wait_recv()
            rim(True, q)

        @pl.when(has_next)
        def _():
            ax_copy(False, q).wait_recv()
            rim(False, q)

    def drain(c, carry):
        for d in range(1, n_az):
            az_copy(d, c).wait_send()
        return carry

    lax.fori_loop(0, count, drain, 0)
    for q in range(CUTS):
        pl.when(up_direct(q))(lambda: ax_copy(True, q).wait_send())
        pl.when(down_direct(q))(lambda: ax_copy(False, q).wait_send())
    for q in hops:
        pl.when(q < hop_up)(lambda: hop_copy(True, q).wait_send())
        pl.when(q < hop_down)(lambda: hop_copy(False, q).wait_send())
        pl.when(q < pass_up)(lambda: pass_copy(True, q).wait_send())
        pl.when(q < pass_down)(lambda: pass_copy(False, q).wait_send())
    for k in range(2):
        pl.when(has_high)(lambda: rad_copy(True, k).wait_send())
        pl.when(has_low)(lambda: rad_copy(False, k).wait_send())
    pl.when(has_prev)(lambda: ax_copy(True, CUTS - 1).wait_recv())
    pl.when(has_next)(lambda: ax_copy(False, CUTS - 1).wait_recv())


def write_kernel(ns, nst, late, coef, out_state, out_section, fin, sem, last_sem):
    _, count, rows, _ = ns.shape
    cut = rows // CUTS
    done = rows - cut
    ends = pl.ds(done, cut)
    rims = sorted({*range(min(HALO, count)), *range(max(count - HALO, 0), count)})
    pairs = ((ns, out_section), (nst, out_state))
    copies = []
    for c in range(count):
        lines = pl.ds(0, done if c in rims else rows)
        for i, (source, target) in enumerate(pairs):
            copies.append(
                pltpu.make_async_copy(source.at[:, c, lines], target.at[:, c, lines], sem.at[i, c])
            )
    for copy in copies:
        copy.start()
    for slot, p in enumerate(rims):
        more = [0.0] * 5
        if p < HALO:
            more = [a + b for a, b in zip(more, rim_terms(late, 0, slice(None), coef, ends, p))]
        if p >= count - HALO:
            more = [a + b for a, b in zip(more, rim_terms(late, 1, slice(None), coef, ends, count - 1 - p))]
        for f in range(5):
            fin[0, f, slot] = ns[f, p, ends] + more[f]
            fin[1, f, slot] = nst[f, p, ends] + section_gain * more[f]
        for i, (_, target) in enumerate(pairs):
            copies.append(
                pltpu.make_async_copy(fin.at[i, :, slot], target.at[:, p, ends], last_sem.at[i, slot])
            )
            copies[-1].start()
    for copy in copies:
        copy.wait()


def body(mesh_sizes, state, section, mean_axial, mean_swirl, mean_density, sound_squared):
    n_ax, n_az, n_rad = mesh_sizes
    _, count, rows, local = state.shape
    near_t = jnp.asarray(near_table(local))
    into_t, outof_t = (jnp.asarray(table) for table in far_tables(n_az, local))
    whole = (5, count, rows, local)
    far = pl.BlockSpec(memory_space=pltpu.HBM)
    near = pl.BlockSpec(memory_space=pltpu.VMEM)
    f32 = jnp.float32
    dma = pltpu.SemaphoreType.DMA
    pin = functools.partial(pltpu.with_memory_space_constraint, memory_space=pltpu.HBM)
    cut = rows // CUTS
    edge = (2, 5, HALO, cut, local)
    ns, nst, late, coef = pl.pallas_call(
        functools.partial(kernel, (n_ax, n_az, n_rad, count, rows, local)),
        out_shape=tuple(pltpu.VMEM(shape, f32) for shape in (whole, whole, edge, (8, rows, local))),
        in_specs=[far] * 9,
        out_specs=(near,) * 4,
        scratch_shapes=[
            pltpu.VMEM((5, count + 2 * HALO, rows, local), f32),
            pltpu.VMEM((2, count, rows + 2 * RIM, local), f32),
            pltpu.VMEM((2, 5, HALO, rows - cut, local), f32),
            pltpu.VMEM((CUTS - 1, 5, HALO, cut, local), f32),
            pltpu.VMEM((5, count, rows, WIDTH), f32),
            pltpu.VMEM((n_az - 1, 5, count, rows, WIDTH), f32),
            pltpu.VMEM((2, local, local), jnp.bfloat16),
            pltpu.VMEM((2, local, WIDTH), jnp.bfloat16),
            pltpu.VMEM((n_az - 1, 2, WIDTH, local), jnp.bfloat16),
            pltpu.VMEM((4, 1, rows), f32),
            dma((11,)),
            dma((n_az - 1, count)),
            dma((n_az - 1, count)),
            dma((2, CUTS)),
            dma((2, CUTS)),
            dma((CUTS - 1,)),
            dma((CUTS - 1,)),
            dma((CUTS - 1,)),
            dma((2, 2)),
            dma((2, 2)),
        ],
        compiler_params=pltpu.CompilerParams(
            collective_id=0, has_side_effects=True, vmem_limit_bytes=36 * 2**20
        ),
        cost_estimate=pl.CostEstimate(
            flops=6 * 5 * count * rows * local * NT,
            bytes_accessed=4 * 4 * 5 * count * rows * local,
            transcendentals=0,
        ),
    )(
        pin(state),
        pin(section),
        pin(mean_axial[None]),
        pin(mean_swirl[None]),
        pin(mean_density[None]),
        pin(sound_squared[None]),
        pin(near_t),
        pin(into_t),
        pin(outof_t),
    )
    return pl.pallas_call(
        write_kernel,
        out_shape=(jax.ShapeDtypeStruct(whole, f32), jax.ShapeDtypeStruct(whole, f32)),
        in_specs=[near] * 4,
        out_specs=(far, far),
        scratch_shapes=[
            pltpu.VMEM((2, 5, min(2 * HALO, count), cut, local), f32),
            dma((2, count)),
            dma((2, min(2 * HALO, count))),
        ],
        compiler_params=pltpu.CompilerParams(vmem_limit_bytes=4 * 2**20),
    )(ns, nst, late, coef)


def solution(mesh):
    spec = P(None, "ax", "rad", "az")
    sizes = (mesh.shape["ax"], mesh.shape["az"], mesh.shape["rad"])
    return jax.shard_map(
        functools.partial(body, sizes),
        mesh=mesh,
        in_specs=(spec, spec, P("rad"), P("rad"), P("rad"), P("rad")),
        out_specs=(spec, spec),
        check_vma=False,
    )
```

```python
import functools
import math

import jax
import jax.numpy as jnp
import numpy as np
from jax import lax
from jax.experimental import pallas as pl
from jax.experimental.pallas import tpu as pltpu
from jax.sharding import PartitionSpec as P

NT = 1024
MESH = pl.DeviceIdType.MESH

drp_coeffs = (0.770882380518, -0.166705904415, 0.02084314277)
section_keep = -0.4178904745
section_gain = 0.3792103129999
time_step = 0.25
HALO = 3
RIM = 8
CUTS = 4
NODES = 64
WIDTH = 2 * NODES


def split(full):
    full = full.astype(np.float32)
    high = full.astype(jnp.bfloat16)
    low = (full - high.astype(np.float32)).astype(jnp.bfloat16)
    return np.stack([high, low])


def near_table(local):
    s = np.arange(local)[:, None]
    t = np.arange(local)[None, :]
    spacing = t - s
    angle = np.pi * spacing / NT
    safe = np.where(spacing == 0, 1.0, np.sin(angle))
    parity = 1.0 - 2.0 * (spacing % 2)
    return split(np.where(spacing == 0, 0.0, 0.5 * parity * np.cos(angle) / safe))


def quadrature():
    step = 0.16
    u = (np.arange(NODES) + 0.5) * step
    scale = 2.0 * np.pi / NT
    t = scale * np.sinh(u)
    weight = step * scale * np.cosh(u) * (NT / np.pi) / -np.expm1(-NT * t)
    return t, weight


def far_tables(owners, local):
    t, weight = quadrature()
    k = np.arange(local)[:, None]
    sign = 1.0 - 2.0 * (k % 2)
    into = np.concatenate([sign * np.exp(-k * t), sign * np.exp(-(local - 1 - k) * t)], axis=1)
    t, weight = t[:, None], weight[:, None]
    j = np.arange(local)[None, :]
    sign = 1.0 - 2.0 * (j % 2)
    outof = []
    for d in range(1, owners):
        below = -0.5 * sign * weight * np.exp(-(NT - d * local - j) * t)
        above = 0.5 * sign * weight * np.exp(-(d * local + j - local + 1) * t)
        outof.append(split(np.concatenate([below, above], axis=0)))
    return split(into), np.stack(outof)


def product(values, high_table, low_table):
    high = values.astype(jnp.bfloat16)
    low = (values - high.astype(jnp.float32)).astype(jnp.bfloat16)
    dot = functools.partial(jnp.dot, preferred_element_type=jnp.float32)
    return dot(high, high_table) + dot(low, high_table) + dot(high, low_table)


def rim_terms(halo, way, lines, coef, rows, reach):
    grads = []
    for f in range(5):
        total = 0.0
        for j in range(reach + 1, HALO + 1):
            past = j - reach - 1
            total += drp_coeffs[j - 1] * halo[way, f, past if way else HALO - 1 - past, lines]
        grads.append(total if way else -total)
    speed, dense, stiff, inverse = coef[0, rows], coef[2, rows], coef[3, rows], coef[4, rows]
    return (
        speed * grads[0] + dense * grads[1],
        speed * grads[1] + inverse * grads[4],
        speed * grads[2],
        speed * grads[3],
        speed * grads[4] + stiff * grads[1],
    )


def kernel(
    sizes, state, section, axial_speed, swirl, density_in, sound, near_in, into_in, outof_in, ns, nst, late, coef,
    st, pr, halo, relay, sums, other, near, into, outof, means,
    load_sem, az_send, az_recv, ax_send, ax_recv, hop_send, hop_recv, pass_send, rad_send, rad_recv,
):
    n_ax, n_az, n_rad, count, rows, local = sizes
    cut = rows // CUTS
    ax = lax.axis_index("ax")
    az = lax.axis_index("az")
    rad = lax.axis_index("rad")
    has_prev, has_next = ax > 0, ax < n_ax - 1
    has_low, has_high = rad > 0, rad < n_rad - 1

    levels = n_ax // 2 if n_ax % 2 == 0 and n_ax <= 2 * CUTS else 0
    level = lax.div(ax, 2)
    odd = lax.rem(ax, 2) == 1
    even = jnp.logical_not(odd)
    zero = jnp.int32(0)
    if levels:
        rest = lax.div((levels - 1 - level) * CUTS, levels)
        gone = lax.div(level * CUTS, levels)
        hop_up = jnp.where(jnp.logical_and(odd, has_next), rest, zero)
        hop_down = jnp.where(jnp.logical_and(even, has_prev), gone, zero)
        pass_up = jnp.where(jnp.logical_and(even, ax + 2 < n_ax), rest, zero)
        pass_down = jnp.where(jnp.logical_and(odd, ax >= 3), gone, zero)
    else:
        hop_up = hop_down = pass_up = pass_down = zero
    hops = range(CUTS - 1 if levels else 0)

    half = count // 2

    def az_copy(d, g):
        planes = pl.ds(g * half, half if g == 0 else count - half)
        return pltpu.make_async_remote_copy(
            src_ref=sums.at[:, planes],
            dst_ref=other.at[d - 1, :, planes],
            send_sem=az_send.at[d - 1, g],
            recv_sem=az_recv.at[d - 1, g],
            device_id={"az": lax.rem(az + d, n_az)},
            device_id_type=MESH,
        )

    def edge(up, q):
        return state.at[:, pl.ds(count - HALO if up else 0, HALO), pl.ds(q * cut, cut)]

    def landing(up, q):
        way = 0 if up else 1
        return late.at[way] if q == CUTS - 1 else halo.at[way, :, :, pl.ds(q * cut, cut)]

    def ax_copy(up, q):
        way = 0 if up else 1
        return pltpu.make_async_remote_copy(
            src_ref=edge(up, q),
            dst_ref=landing(up, q),
            send_sem=ax_send.at[way, q],
            recv_sem=ax_recv.at[way, q],
            device_id={"ax": ax + 1 if up else ax - 1},
            device_id_type=MESH,
        )

    def hop_copy(up, q):
        return pltpu.make_async_remote_copy(
            src_ref=edge(up, q),
            dst_ref=relay.at[q],
            send_sem=hop_send.at[q],
            recv_sem=hop_recv.at[q],
            device_id={"ax": ax - 1 if up else ax + 1},
            device_id_type=MESH,
        )

    def pass_copy(up, q):
        return pltpu.make_async_remote_copy(
            src_ref=relay.at[q],
            dst_ref=landing(up, q),
            send_sem=pass_send.at[q],
            recv_sem=ax_recv.at[0 if up else 1, q],
            device_id={"ax": ax + 2 if up else ax - 2},
            device_id_type=MESH,
        )

    def rad_copy(up, k):
        return pltpu.make_async_remote_copy(
            src_ref=state.at[2 + 2 * k, :, pl.ds(rows - RIM if up else 0, RIM)],
            dst_ref=pr.at[k, :, pl.ds(0 if up else rows + RIM, RIM)],
            send_sem=rad_send.at[0 if up else 1, k],
            recv_sem=rad_recv.at[0 if up else 1, k],
            device_id={"rad": rad + 1 if up else rad - 1},
            device_id_type=MESH,
        )

    loads = [
        pltpu.make_async_copy(state, st.at[:, pl.ds(HALO, count)], load_sem.at[0]),
        pltpu.make_async_copy(into_in, into, load_sem.at[1]),
        pltpu.make_async_copy(section, ns, load_sem.at[2]),
        pltpu.make_async_copy(state.at[2], pr.at[0, :, pl.ds(RIM, rows)], load_sem.at[3]),
        pltpu.make_async_copy(state.at[4], pr.at[1, :, pl.ds(RIM, rows)], load_sem.at[4]),
        pltpu.make_async_copy(near_in, near, load_sem.at[5]),
        pltpu.make_async_copy(outof_in, outof, load_sem.at[6]),
    ]
    vectors = [
        pltpu.make_async_copy(ref, means.at[i], load_sem.at[7 + i])
        for i, ref in enumerate((axial_speed, swirl, density_in, sound))
    ]

    barrier = pltpu.get_barrier_semaphore()

    def greet(axis, index):
        pl.semaphore_signal(barrier, inc=1, device_id={axis: index}, device_id_type=MESH)

    met = zero + (n_az - 1)
    for d in (-2, -1, 1, 2) if levels else (-1, 1):
        there = jnp.logical_and(ax + d >= 0, ax + d < n_ax)
        pl.when(there)(lambda: greet("ax", ax + d))
        met = met + there.astype(jnp.int32)
    for d in range(1, n_az):
        greet("az", lax.rem(az + d, n_az))
    pl.when(has_low)(lambda: greet("rad", rad - 1))
    pl.when(has_high)(lambda: greet("rad", rad + 1))
    met = met + has_low.astype(jnp.int32) + has_high.astype(jnp.int32)
    pl.semaphore_wait(barrier, met)

    up_direct = lambda q: jnp.logical_and(has_next, q >= hop_up)
    down_direct = lambda q: jnp.logical_and(has_prev, q >= hop_down)

    def send(q, first):
        up = jnp.logical_and(up_direct(q), odd if first else even)
        down = jnp.logical_and(down_direct(q), even if first else odd)
        pl.when(up)(lambda: ax_copy(True, q).start())
        pl.when(down)(lambda: ax_copy(False, q).start())

    for q in hops:
        pl.when(q < hop_up)(lambda: hop_copy(True, q).start())
        pl.when(q < hop_down)(lambda: hop_copy(False, q).start())
    for first in (True, False):
        for q in range(CUTS):
            send(q, first)
    for k in range(2):
        pl.when(has_high)(lambda: rad_copy(True, k).start())
        pl.when(has_low)(lambda: rad_copy(False, k).start())

    for copy in vectors + loads:
        copy.start()
    for copy in vectors:
        copy.wait()

    pick = lax.broadcasted_iota(jnp.int32, (rows, rows), 0) == lax.broadcasted_iota(
        jnp.int32, (rows, rows), 1
    )

    def column(i):
        line = jnp.broadcast_to(means[i], (rows, rows))
        return jnp.sum(jnp.where(pick, line, 0.0), axis=1, keepdims=True)

    cell = lax.broadcasted_iota(jnp.int32, (rows, local), 0) + rad * rows
    inv_radius = 1.0 / (NT / (2.0 * math.pi) + cell.astype(jnp.float32) + 0.5)
    density = jnp.broadcast_to(column(2), (rows, local))
    minus = -time_step
    inverse = minus / density
    stiff = minus * density * column(3)
    coef[0] = jnp.broadcast_to(minus * column(0), (rows, local))
    coef[1] = minus * column(1) * inv_radius
    coef[2] = minus * density
    coef[3] = stiff
    coef[4] = inverse
    coef[5] = minus * density * inv_radius
    coef[6] = stiff * inv_radius
    coef[7] = inverse * inv_radius

    for copy in loads[:2]:
        copy.wait()

    def gather(c, carry):
        flat = st[:, HALO + c].reshape(5 * rows, local)
        sums[:, c] = product(flat, into[0], into[1]).reshape(5, rows, WIDTH)
        return carry

    for g, (start, stop) in enumerate(((0, half), (half, count))):
        lax.fori_loop(start, stop, gather, 0)
        for d in range(1, n_az):
            az_copy(d, g).start()

    for start in (0, count + HALO):
        st[:, pl.ds(start, HALO)] = jnp.zeros((5, HALO, rows, local), jnp.float32)

    for copy in loads[2:]:
        copy.wait()

    def wall(low):
        def fill(c, carry):
            for k, sign in enumerate((-1.0, 1.0)):
                for j in range(3):
                    if low:
                        pr[k, c, pl.ds(RIM - 1 - j, 1)] = sign * pr[k, c, pl.ds(RIM + j, 1)]
                    else:
                        pr[k, c, pl.ds(RIM + rows + j, 1)] = sign * pr[
                            k, c, pl.ds(RIM + rows - 1 - j, 1)
                        ]
            return carry

        lax.fori_loop(0, count, fill, 0)

    pl.when(jnp.logical_not(has_low))(lambda: wall(True))
    pl.when(jnp.logical_not(has_high))(lambda: wall(False))
    for k in range(2):
        pl.when(has_low)(lambda: rad_copy(True, k).wait_recv())
        pl.when(has_high)(lambda: rad_copy(False, k).wait_recv())

    def radial(k, c):
        total = jnp.zeros((rows, local), jnp.float32)
        for j in range(1, 4):
            total += drp_coeffs[j - 1] * (
                pr[k, c, pl.ds(RIM + j, rows)] - pr[k, c, pl.ds(RIM - j, rows)]
            )
        return total

    def axial(f, c):
        total = jnp.zeros((rows, local), jnp.float32)
        for j in range(1, 4):
            total += drp_coeffs[j - 1] * (st[f, c + HALO + j] - st[f, c + HALO - j])
        return total

    for way, there in enumerate((has_prev, has_next)):
        @pl.when(jnp.logical_not(there))
        def _():
            late[way] = jnp.zeros_like(late[way])

    def pass_on(q):
        @pl.when(q < pass_up)
        def _():
            hop_copy(True, q).wait_recv()
            pass_copy(True, q).start()

        @pl.when(q < pass_down)
        def _():
            hop_copy(False, q).wait_recv()
            pass_copy(False, q).start()

    def plane(c, carry):
        spread = radial(0, c)
        along = axial(1, c)
        press = axial(4, c)
        speed = coef[0]
        ns[0, c] = section_keep * ns[0, c] + speed * axial(0, c) + coef[2] * (along + spread)
        ns[1, c] = section_keep * ns[1, c] + speed * along + coef[4] * press
        ns[2, c] = section_keep * ns[2, c] + speed * axial(2, c) + coef[4] * radial(1, c)
        ns[3, c] = section_keep * ns[3, c] + speed * axial(3, c)
        ns[4, c] = section_keep * ns[4, c] + speed * press + coef[3] * (along + spread)
        @pl.when(c == 0)
        def _():
            for d in range(1, n_az):
                az_copy(d, 0).wait_recv()

        @pl.when(c == half)
        def _():
            for d in range(1, n_az):
                az_copy(d, 1).wait_recv()

        g = product(st[:, HALO + c].reshape(5 * rows, local), near[0], near[1])
        for d in range(1, n_az):
            g += product(other[d - 1, :, c].reshape(5 * rows, WIDTH), outof[d - 1, 0], outof[d - 1, 1])
        g = g.reshape(5, rows, local)
        rate = coef[1]
        ns[0, c] += rate * g[0] + coef[5] * g[3]
        ns[1, c] += rate * g[1]
        ns[2, c] += rate * g[2]
        ns[3, c] += rate * g[3] + coef[7] * g[4]
        ns[4, c] += rate * g[4] + coef[6] * g[3]
        for f in range(5):
            nst[f, c] = st[f, HALO + c] + section_gain * ns[f, c]
        for q in hops:
            pl.when(c == min(2 * q + 1, count - 1))(lambda: pass_on(q))
        return carry

    lax.fori_loop(0, count, plane, 0)

    def rim(up, q):
        lines = pl.ds(q * cut, cut)
        for reach in range(HALO):
            p = reach if up else count - 1 - reach
            more = rim_terms(halo, 0 if up else 1, lines, coef, lines, reach)
            for f in range(5):
                value = ns[f, p, lines] + more[f]
                ns[f, p, lines] = value
                nst[f, p, lines] = st[f, HALO + p, lines] + section_gain * value

    for q in range(CUTS - 1):
        @pl.when(has_prev)
        def _():
            ax_copy(True, q).wait_recv()
            rim(True, q)

        @pl.when(has_next)
        def _():
            ax_copy(False, q).wait_recv()
            rim(False, q)

    for d in range(1, n_az):
        for g in range(2):
            az_copy(d, g).wait_send()
    for q in range(CUTS):
        pl.when(up_direct(q))(lambda: ax_copy(True, q).wait_send())
        pl.when(down_direct(q))(lambda: ax_copy(False, q).wait_send())
    for q in hops:
        pl.when(q < hop_up)(lambda: hop_copy(True, q).wait_send())
        pl.when(q < hop_down)(lambda: hop_copy(False, q).wait_send())
        pl.when(q < pass_up)(lambda: pass_copy(True, q).wait_send())
        pl.when(q < pass_down)(lambda: pass_copy(False, q).wait_send())
    for k in range(2):
        pl.when(has_high)(lambda: rad_copy(True, k).wait_send())
        pl.when(has_low)(lambda: rad_copy(False, k).wait_send())
    pl.when(has_prev)(lambda: ax_copy(True, CUTS - 1).wait_recv())
    pl.when(has_next)(lambda: ax_copy(False, CUTS - 1).wait_recv())


def write_kernel(ns, nst, late, coef, out_state, out_section, fin, sem, last_sem):
    _, count, rows, _ = ns.shape
    cut = rows // CUTS
    done = rows - cut
    ends = pl.ds(done, cut)
    rims = sorted({*range(min(HALO, count)), *range(max(count - HALO, 0), count)})
    pairs = ((ns, out_section), (nst, out_state))
    copies = []
    for c in range(count):
        lines = pl.ds(0, done if c in rims else rows)
        for i, (source, target) in enumerate(pairs):
            copies.append(
                pltpu.make_async_copy(source.at[:, c, lines], target.at[:, c, lines], sem.at[i, c])
            )
    for copy in copies:
        copy.start()
    for slot, p in enumerate(rims):
        more = [0.0] * 5
        if p < HALO:
            more = [a + b for a, b in zip(more, rim_terms(late, 0, slice(None), coef, ends, p))]
        if p >= count - HALO:
            more = [a + b for a, b in zip(more, rim_terms(late, 1, slice(None), coef, ends, count - 1 - p))]
        for f in range(5):
            fin[0, f, slot] = ns[f, p, ends] + more[f]
            fin[1, f, slot] = nst[f, p, ends] + section_gain * more[f]
        for i, (_, target) in enumerate(pairs):
            copies.append(
                pltpu.make_async_copy(fin.at[i, :, slot], target.at[:, p, ends], last_sem.at[i, slot])
            )
            copies[-1].start()
    for copy in copies:
        copy.wait()


def body(mesh_sizes, state, section, mean_axial, mean_swirl, mean_density, sound_squared):
    n_ax, n_az, n_rad = mesh_sizes
    _, count, rows, local = state.shape
    near_t = jnp.asarray(near_table(local))
    into_t, outof_t = (jnp.asarray(table) for table in far_tables(n_az, local))
    whole = (5, count, rows, local)
    far = pl.BlockSpec(memory_space=pltpu.HBM)
    near = pl.BlockSpec(memory_space=pltpu.VMEM)
    f32 = jnp.float32
    dma = pltpu.SemaphoreType.DMA
    pin = functools.partial(pltpu.with_memory_space_constraint, memory_space=pltpu.HBM)
    cut = rows // CUTS
    edge = (2, 5, HALO, cut, local)
    ns, nst, late, coef = pl.pallas_call(
        functools.partial(kernel, (n_ax, n_az, n_rad, count, rows, local)),
        out_shape=tuple(pltpu.VMEM(shape, f32) for shape in (whole, whole, edge, (8, rows, local))),
        in_specs=[far] * 9,
        out_specs=(near,) * 4,
        scratch_shapes=[
            pltpu.VMEM((5, count + 2 * HALO, rows, local), f32),
            pltpu.VMEM((2, count, rows + 2 * RIM, local), f32),
            pltpu.VMEM((2, 5, HALO, rows - cut, local), f32),
            pltpu.VMEM((CUTS - 1, 5, HALO, cut, local), f32),
            pltpu.VMEM((5, count, rows, WIDTH), f32),
            pltpu.VMEM((n_az - 1, 5, count, rows, WIDTH), f32),
            pltpu.VMEM((2, local, local), jnp.bfloat16),
            pltpu.VMEM((2, local, WIDTH), jnp.bfloat16),
            pltpu.VMEM((n_az - 1, 2, WIDTH, local), jnp.bfloat16),
            pltpu.VMEM((4, 1, rows), f32),
            dma((11,)),
            dma((n_az - 1, 2)),
            dma((n_az - 1, 2)),
            dma((2, CUTS)),
            dma((2, CUTS)),
            dma((CUTS - 1,)),
            dma((CUTS - 1,)),
            dma((CUTS - 1,)),
            dma((2, 2)),
            dma((2, 2)),
        ],
        compiler_params=pltpu.CompilerParams(
            collective_id=0, has_side_effects=True, vmem_limit_bytes=36 * 2**20
        ),
        cost_estimate=pl.CostEstimate(
            flops=6 * 5 * count * rows * local * NT,
            bytes_accessed=4 * 4 * 5 * count * rows * local,
            transcendentals=0,
        ),
    )(
        pin(state),
        pin(section),
        pin(mean_axial[None]),
        pin(mean_swirl[None]),
        pin(mean_density[None]),
        pin(sound_squared[None]),
        pin(near_t),
        pin(into_t),
        pin(outof_t),
    )
    return pl.pallas_call(
        write_kernel,
        out_shape=(jax.ShapeDtypeStruct(whole, f32), jax.ShapeDtypeStruct(whole, f32)),
        in_specs=[near] * 4,
        out_specs=(far, far),
        scratch_shapes=[
            pltpu.VMEM((2, 5, min(2 * HALO, count), cut, local), f32),
            dma((2, count)),
            dma((2, min(2 * HALO, count))),
        ],
        compiler_params=pltpu.CompilerParams(vmem_limit_bytes=4 * 2**20),
    )(ns, nst, late, coef)


def solution(mesh):
    spec = P(None, "ax", "rad", "az")
    sizes = (mesh.shape["ax"], mesh.shape["az"], mesh.shape["rad"])
    return jax.shard_map(
        functools.partial(body, sizes),
        mesh=mesh,
        in_specs=(spec, spec, P("rad"), P("rad"), P("rad"), P("rad")),
        out_specs=(spec, spec),
        check_vma=False,
    )
```

```python
import functools
import math

import jax
import jax.numpy as jnp
import numpy as np
from jax import lax
from jax.experimental import pallas as pl
from jax.experimental.pallas import tpu as pltpu
from jax.sharding import PartitionSpec as P

NT = 1024
MESH = pl.DeviceIdType.MESH

drp_coeffs = (0.770882380518, -0.166705904415, 0.02084314277)
section_keep = -0.4178904745
section_gain = 0.3792103129999
time_step = 0.25
HALO = 3
RIM = 8
CUTS = 4
NODES = 64
WIDTH = 2 * NODES


def split(full):
    full = full.astype(np.float32)
    high = full.astype(jnp.bfloat16)
    low = (full - high.astype(np.float32)).astype(jnp.bfloat16)
    return np.stack([high, low])


def near_table(local):
    s = np.arange(local)[:, None]
    t = np.arange(local)[None, :]
    spacing = t - s
    angle = np.pi * spacing / NT
    safe = np.where(spacing == 0, 1.0, np.sin(angle))
    parity = 1.0 - 2.0 * (spacing % 2)
    return split(np.where(spacing == 0, 0.0, 0.5 * parity * np.cos(angle) / safe))


def quadrature():
    step = 0.16
    u = (np.arange(NODES) + 0.5) * step
    scale = 2.0 * np.pi / NT
    t = scale * np.sinh(u)
    weight = step * scale * np.cosh(u) * (NT / np.pi) / -np.expm1(-NT * t)
    return t, weight


def far_tables(owners, local):
    t, weight = quadrature()
    k = np.arange(local)[:, None]
    sign = 1.0 - 2.0 * (k % 2)
    into = np.concatenate([sign * np.exp(-k * t), sign * np.exp(-(local - 1 - k) * t)], axis=1)
    t, weight = t[:, None], weight[:, None]
    j = np.arange(local)[None, :]
    sign = 1.0 - 2.0 * (j % 2)
    outof = []
    for d in range(1, owners):
        below = -0.5 * sign * weight * np.exp(-(NT - d * local - j) * t)
        above = 0.5 * sign * weight * np.exp(-(d * local + j - local + 1) * t)
        outof.append(split(np.concatenate([below, above], axis=0)))
    return split(into), np.stack(outof)


def product(values, high_table, low_table):
    high = values.astype(jnp.bfloat16)
    low = (values - high.astype(jnp.float32)).astype(jnp.bfloat16)
    dot = functools.partial(jnp.dot, preferred_element_type=jnp.float32)
    return dot(high, high_table) + dot(low, high_table) + dot(high, low_table)


def rim_terms(halo, way, lines, coef, rows, reach):
    grads = []
    for f in range(5):
        total = 0.0
        for j in range(reach + 1, HALO + 1):
            past = j - reach - 1
            total += drp_coeffs[j - 1] * halo[way, f, past if way else HALO - 1 - past, lines]
        grads.append(total if way else -total)
    speed, dense, stiff, inverse = coef[0, rows], coef[2, rows], coef[3, rows], coef[4, rows]
    return (
        speed * grads[0] + dense * grads[1],
        speed * grads[1] + inverse * grads[4],
        speed * grads[2],
        speed * grads[3],
        speed * grads[4] + stiff * grads[1],
    )


def kernel(
    sizes, state, section, axial_speed, swirl, density_in, sound, near_in, into_in, outof_in, ns, nst, late, coef,
    st, pr, halo, relay, sums, other, near, into, outof, means,
    load_sem, az_send, az_recv, ax_send, ax_recv, hop_send, hop_recv, pass_send, rad_send, rad_recv,
):
    n_ax, n_az, n_rad, count, rows, local = sizes
    cut = rows // CUTS
    ax = lax.axis_index("ax")
    az = lax.axis_index("az")
    rad = lax.axis_index("rad")
    has_prev, has_next = ax > 0, ax < n_ax - 1
    has_low, has_high = rad > 0, rad < n_rad - 1

    levels = n_ax // 2 if n_ax % 2 == 0 and n_ax <= 2 * CUTS else 0
    level = lax.div(ax, 2)
    odd = lax.rem(ax, 2) == 1
    even = jnp.logical_not(odd)
    zero = jnp.int32(0)
    if levels:
        rest = lax.div((levels - 1 - level) * CUTS, levels)
        gone = lax.div(level * CUTS, levels)
        hop_up = jnp.where(jnp.logical_and(odd, has_next), rest, zero)
        hop_down = jnp.where(jnp.logical_and(even, has_prev), gone, zero)
        pass_up = jnp.where(jnp.logical_and(even, ax + 2 < n_ax), rest, zero)
        pass_down = jnp.where(jnp.logical_and(odd, ax >= 3), gone, zero)
    else:
        hop_up = hop_down = pass_up = pass_down = zero
    hops = range(CUTS - 1 if levels else 0)

    half = count // 2

    def az_copy(d, g):
        planes = pl.ds(g * half, half if g == 0 else count - half)
        return pltpu.make_async_remote_copy(
            src_ref=sums.at[:, planes],
            dst_ref=other.at[d - 1, :, planes],
            send_sem=az_send.at[d - 1, g],
            recv_sem=az_recv.at[d - 1, g],
            device_id={"az": lax.rem(az + d, n_az)},
            device_id_type=MESH,
        )

    def edge(up, q):
        return state.at[:, pl.ds(count - HALO if up else 0, HALO), pl.ds(q * cut, cut)]

    def landing(up, q):
        way = 0 if up else 1
        return late.at[way] if q == CUTS - 1 else halo.at[way, :, :, pl.ds(q * cut, cut)]

    def ax_copy(up, q):
        way = 0 if up else 1
        return pltpu.make_async_remote_copy(
            src_ref=edge(up, q),
            dst_ref=landing(up, q),
            send_sem=ax_send.at[way, q],
            recv_sem=ax_recv.at[way, q],
            device_id={"ax": ax + 1 if up else ax - 1},
            device_id_type=MESH,
        )

    def hop_copy(up, q):
        return pltpu.make_async_remote_copy(
            src_ref=edge(up, q),
            dst_ref=relay.at[q],
            send_sem=hop_send.at[q],
            recv_sem=hop_recv.at[q],
            device_id={"ax": ax - 1 if up else ax + 1},
            device_id_type=MESH,
        )

    def pass_copy(up, q):
        return pltpu.make_async_remote_copy(
            src_ref=relay.at[q],
            dst_ref=landing(up, q),
            send_sem=pass_send.at[q],
            recv_sem=ax_recv.at[0 if up else 1, q],
            device_id={"ax": ax + 2 if up else ax - 2},
            device_id_type=MESH,
        )

    def rad_copy(up, k):
        return pltpu.make_async_remote_copy(
            src_ref=state.at[2 + 2 * k, :, pl.ds(rows - RIM if up else 0, RIM)],
            dst_ref=pr.at[k, :, pl.ds(0 if up else rows + RIM, RIM)],
            send_sem=rad_send.at[0 if up else 1, k],
            recv_sem=rad_recv.at[0 if up else 1, k],
            device_id={"rad": rad + 1 if up else rad - 1},
            device_id_type=MESH,
        )

    loads = [
        pltpu.make_async_copy(state, st.at[:, pl.ds(HALO, count)], load_sem.at[0]),
        pltpu.make_async_copy(into_in, into, load_sem.at[1]),
        pltpu.make_async_copy(section, ns, load_sem.at[2]),
        pltpu.make_async_copy(state.at[2], pr.at[0, :, pl.ds(RIM, rows)], load_sem.at[3]),
        pltpu.make_async_copy(state.at[4], pr.at[1, :, pl.ds(RIM, rows)], load_sem.at[4]),
        pltpu.make_async_copy(near_in, near, load_sem.at[5]),
        pltpu.make_async_copy(outof_in, outof, load_sem.at[6]),
    ]
    vectors = [
        pltpu.make_async_copy(ref, means.at[i], load_sem.at[7 + i])
        for i, ref in enumerate((axial_speed, swirl, density_in, sound))
    ]

    barrier = pltpu.get_barrier_semaphore()

    def greet(axis, index):
        pl.semaphore_signal(barrier, inc=1, device_id={axis: index}, device_id_type=MESH)

    met = zero + (n_az - 1)
    for d in (-2, -1, 1, 2) if levels else (-1, 1):
        there = jnp.logical_and(ax + d >= 0, ax + d < n_ax)
        pl.when(there)(lambda: greet("ax", ax + d))
        met = met + there.astype(jnp.int32)
    for d in range(1, n_az):
        greet("az", lax.rem(az + d, n_az))
    pl.when(has_low)(lambda: greet("rad", rad - 1))
    pl.when(has_high)(lambda: greet("rad", rad + 1))
    met = met + has_low.astype(jnp.int32) + has_high.astype(jnp.int32)
    pl.semaphore_wait(barrier, met)

    up_direct = lambda q: jnp.logical_and(has_next, q >= hop_up)
    down_direct = lambda q: jnp.logical_and(has_prev, q >= hop_down)

    def send(q, first):
        up = jnp.logical_and(up_direct(q), odd if first else even)
        down = jnp.logical_and(down_direct(q), even if first else odd)
        pl.when(up)(lambda: ax_copy(True, q).start())
        pl.when(down)(lambda: ax_copy(False, q).start())

    for q in hops:
        pl.when(q < hop_up)(lambda: hop_copy(True, q).start())
        pl.when(q < hop_down)(lambda: hop_copy(False, q).start())
    for first in (True, False):
        for q in range(CUTS):
            send(q, first)
    for k in range(2):
        pl.when(has_high)(lambda: rad_copy(True, k).start())
        pl.when(has_low)(lambda: rad_copy(False, k).start())

    for copy in vectors + loads[:2]:
        copy.start()
    for copy in vectors:
        copy.wait()

    pick = lax.broadcasted_iota(jnp.int32, (rows, rows), 0) == lax.broadcasted_iota(
        jnp.int32, (rows, rows), 1
    )

    def column(i):
        line = jnp.broadcast_to(means[i], (rows, rows))
        return jnp.sum(jnp.where(pick, line, 0.0), axis=1, keepdims=True)

    cell = lax.broadcasted_iota(jnp.int32, (rows, local), 0) + rad * rows
    inv_radius = 1.0 / (NT / (2.0 * math.pi) + cell.astype(jnp.float32) + 0.5)
    density = jnp.broadcast_to(column(2), (rows, local))
    minus = -time_step
    inverse = minus / density
    stiff = minus * density * column(3)
    coef[0] = jnp.broadcast_to(minus * column(0), (rows, local))
    coef[1] = minus * column(1) * inv_radius
    coef[2] = minus * density
    coef[3] = stiff
    coef[4] = inverse
    coef[5] = minus * density * inv_radius
    coef[6] = stiff * inv_radius
    coef[7] = inverse * inv_radius

    for copy in loads[:2]:
        copy.wait()

    def gather(c, carry):
        flat = st[:, HALO + c].reshape(5 * rows, local)
        sums[:, c] = product(flat, into[0], into[1]).reshape(5, rows, WIDTH)
        return carry

    for g, (start, stop) in enumerate(((0, half), (half, count))):
        lax.fori_loop(start, stop, gather, 0)
        for d in range(1, n_az):
            az_copy(d, g).start()

    for copy in loads[2:]:
        copy.start()

    for start in (0, count + HALO):
        st[:, pl.ds(start, HALO)] = jnp.zeros((5, HALO, rows, local), jnp.float32)

    for copy in loads[2:]:
        copy.wait()

    def wall(low):
        def fill(c, carry):
            for k, sign in enumerate((-1.0, 1.0)):
                for j in range(3):
                    if low:
                        pr[k, c, pl.ds(RIM - 1 - j, 1)] = sign * pr[k, c, pl.ds(RIM + j, 1)]
                    else:
                        pr[k, c, pl.ds(RIM + rows + j, 1)] = sign * pr[
                            k, c, pl.ds(RIM + rows - 1 - j, 1)
                        ]
            return carry

        lax.fori_loop(0, count, fill, 0)

    pl.when(jnp.logical_not(has_low))(lambda: wall(True))
    pl.when(jnp.logical_not(has_high))(lambda: wall(False))
    for k in range(2):
        pl.when(has_low)(lambda: rad_copy(True, k).wait_recv())
        pl.when(has_high)(lambda: rad_copy(False, k).wait_recv())

    def radial(k, c):
        total = jnp.zeros((rows, local), jnp.float32)
        for j in range(1, 4):
            total += drp_coeffs[j - 1] * (
                pr[k, c, pl.ds(RIM + j, rows)] - pr[k, c, pl.ds(RIM - j, rows)]
            )
        return total

    def axial(f, c):
        total = jnp.zeros((rows, local), jnp.float32)
        for j in range(1, 4):
            total += drp_coeffs[j - 1] * (st[f, c + HALO + j] - st[f, c + HALO - j])
        return total

    for way, there in enumerate((has_prev, has_next)):
        @pl.when(jnp.logical_not(there))
        def _():
            late[way] = jnp.zeros_like(late[way])

    def pass_on(q):
        @pl.when(q < pass_up)
        def _():
            hop_copy(True, q).wait_recv()
            pass_copy(True, q).start()

        @pl.when(q < pass_down)
        def _():
            hop_copy(False, q).wait_recv()
            pass_copy(False, q).start()

    def plane(c, carry):
        spread = radial(0, c)
        along = axial(1, c)
        press = axial(4, c)
        speed = coef[0]
        ns[0, c] = section_keep * ns[0, c] + speed * axial(0, c) + coef[2] * (along + spread)
        ns[1, c] = section_keep * ns[1, c] + speed * along + coef[4] * press
        ns[2, c] = section_keep * ns[2, c] + speed * axial(2, c) + coef[4] * radial(1, c)
        ns[3, c] = section_keep * ns[3, c] + speed * axial(3, c)
        ns[4, c] = section_keep * ns[4, c] + speed * press + coef[3] * (along + spread)
        @pl.when(c == 0)
        def _():
            for d in range(1, n_az):
                az_copy(d, 0).wait_recv()

        @pl.when(c == half)
        def _():
            for d in range(1, n_az):
                az_copy(d, 1).wait_recv()

        g = product(st[:, HALO + c].reshape(5 * rows, local), near[0], near[1])
        for d in range(1, n_az):
            g += product(other[d - 1, :, c].reshape(5 * rows, WIDTH), outof[d - 1, 0], outof[d - 1, 1])
        g = g.reshape(5, rows, local)
        rate = coef[1]
        ns[0, c] += rate * g[0] + coef[5] * g[3]
        ns[1, c] += rate * g[1]
        ns[2, c] += rate * g[2]
        ns[3, c] += rate * g[3] + coef[7] * g[4]
        ns[4, c] += rate * g[4] + coef[6] * g[3]
        for f in range(5):
            nst[f, c] = st[f, HALO + c] + section_gain * ns[f, c]
        for q in hops:
            pl.when(c == min(2 * q + 1, count - 1))(lambda: pass_on(q))
        return carry

    lax.fori_loop(0, count, plane, 0)

    def rim(up, q):
        lines = pl.ds(q * cut, cut)
        for reach in range(HALO):
            p = reach if up else count - 1 - reach
            more = rim_terms(halo, 0 if up else 1, lines, coef, lines, reach)
            for f in range(5):
                value = ns[f, p, lines] + more[f]
                ns[f, p, lines] = value
                nst[f, p, lines] = st[f, HALO + p, lines] + section_gain * value

    for q in range(CUTS - 1):
        @pl.when(has_prev)
        def _():
            ax_copy(True, q).wait_recv()
            rim(True, q)

        @pl.when(has_next)
        def _():
            ax_copy(False, q).wait_recv()
            rim(False, q)

    for d in range(1, n_az):
        for g in range(2):
            az_copy(d, g).wait_send()
    for q in range(CUTS):
        pl.when(up_direct(q))(lambda: ax_copy(True, q).wait_send())
        pl.when(down_direct(q))(lambda: ax_copy(False, q).wait_send())
    for q in hops:
        pl.when(q < hop_up)(lambda: hop_copy(True, q).wait_send())
        pl.when(q < hop_down)(lambda: hop_copy(False, q).wait_send())
        pl.when(q < pass_up)(lambda: pass_copy(True, q).wait_send())
        pl.when(q < pass_down)(lambda: pass_copy(False, q).wait_send())
    for k in range(2):
        pl.when(has_high)(lambda: rad_copy(True, k).wait_send())
        pl.when(has_low)(lambda: rad_copy(False, k).wait_send())
    pl.when(has_prev)(lambda: ax_copy(True, CUTS - 1).wait_recv())
    pl.when(has_next)(lambda: ax_copy(False, CUTS - 1).wait_recv())


def write_kernel(ns, nst, late, coef, out_state, out_section, fin, sem, last_sem):
    _, count, rows, _ = ns.shape
    cut = rows // CUTS
    done = rows - cut
    ends = pl.ds(done, cut)
    rims = sorted({*range(min(HALO, count)), *range(max(count - HALO, 0), count)})
    pairs = ((ns, out_section), (nst, out_state))
    copies = []
    for c in range(count):
        lines = pl.ds(0, done if c in rims else rows)
        for i, (source, target) in enumerate(pairs):
            copies.append(
                pltpu.make_async_copy(source.at[:, c, lines], target.at[:, c, lines], sem.at[i, c])
            )
    for copy in copies:
        copy.start()
    for slot, p in enumerate(rims):
        more = [0.0] * 5
        if p < HALO:
            more = [a + b for a, b in zip(more, rim_terms(late, 0, slice(None), coef, ends, p))]
        if p >= count - HALO:
            more = [a + b for a, b in zip(more, rim_terms(late, 1, slice(None), coef, ends, count - 1 - p))]
        for f in range(5):
            fin[0, f, slot] = ns[f, p, ends] + more[f]
            fin[1, f, slot] = nst[f, p, ends] + section_gain * more[f]
        for i, (_, target) in enumerate(pairs):
            copies.append(
                pltpu.make_async_copy(fin.at[i, :, slot], target.at[:, p, ends], last_sem.at[i, slot])
            )
            copies[-1].start()
    for copy in copies:
        copy.wait()


def body(mesh_sizes, state, section, mean_axial, mean_swirl, mean_density, sound_squared):
    n_ax, n_az, n_rad = mesh_sizes
    _, count, rows, local = state.shape
    near_t = jnp.asarray(near_table(local))
    into_t, outof_t = (jnp.asarray(table) for table in far_tables(n_az, local))
    whole = (5, count, rows, local)
    far = pl.BlockSpec(memory_space=pltpu.HBM)
    near = pl.BlockSpec(memory_space=pltpu.VMEM)
    f32 = jnp.float32
    dma = pltpu.SemaphoreType.DMA
    pin = functools.partial(pltpu.with_memory_space_constraint, memory_space=pltpu.HBM)
    cut = rows // CUTS
    edge = (2, 5, HALO, cut, local)
    ns, nst, late, coef = pl.pallas_call(
        functools.partial(kernel, (n_ax, n_az, n_rad, count, rows, local)),
        out_shape=tuple(pltpu.VMEM(shape, f32) for shape in (whole, whole, edge, (8, rows, local))),
        in_specs=[far] * 9,
        out_specs=(near,) * 4,
        scratch_shapes=[
            pltpu.VMEM((5, count + 2 * HALO, rows, local), f32),
            pltpu.VMEM((2, count, rows + 2 * RIM, local), f32),
            pltpu.VMEM((2, 5, HALO, rows - cut, local), f32),
            pltpu.VMEM((CUTS - 1, 5, HALO, cut, local), f32),
            pltpu.VMEM((5, count, rows, WIDTH), f32),
            pltpu.VMEM((n_az - 1, 5, count, rows, WIDTH), f32),
            pltpu.VMEM((2, local, local), jnp.bfloat16),
            pltpu.VMEM((2, local, WIDTH), jnp.bfloat16),
            pltpu.VMEM((n_az - 1, 2, WIDTH, local), jnp.bfloat16),
            pltpu.VMEM((4, 1, rows), f32),
            dma((11,)),
            dma((n_az - 1, 2)),
            dma((n_az - 1, 2)),
            dma((2, CUTS)),
            dma((2, CUTS)),
            dma((CUTS - 1,)),
            dma((CUTS - 1,)),
            dma((CUTS - 1,)),
            dma((2, 2)),
            dma((2, 2)),
        ],
        compiler_params=pltpu.CompilerParams(
            collective_id=0, has_side_effects=True, vmem_limit_bytes=36 * 2**20
        ),
        cost_estimate=pl.CostEstimate(
            flops=6 * 5 * count * rows * local * NT,
            bytes_accessed=4 * 4 * 5 * count * rows * local,
            transcendentals=0,
        ),
    )(
        pin(state),
        pin(section),
        pin(mean_axial[None]),
        pin(mean_swirl[None]),
        pin(mean_density[None]),
        pin(sound_squared[None]),
        pin(near_t),
        pin(into_t),
        pin(outof_t),
    )
    return pl.pallas_call(
        write_kernel,
        out_shape=(jax.ShapeDtypeStruct(whole, f32), jax.ShapeDtypeStruct(whole, f32)),
        in_specs=[near] * 4,
        out_specs=(far, far),
        scratch_shapes=[
            pltpu.VMEM((2, 5, min(2 * HALO, count), cut, local), f32),
            dma((2, count)),
            dma((2, min(2 * HALO, count))),
        ],
        compiler_params=pltpu.CompilerParams(vmem_limit_bytes=4 * 2**20),
    )(ns, nst, late, coef)


def solution(mesh):
    spec = P(None, "ax", "rad", "az")
    sizes = (mesh.shape["ax"], mesh.shape["az"], mesh.shape["rad"])
    return jax.shard_map(
        functools.partial(body, sizes),
        mesh=mesh,
        in_specs=(spec, spec, P("rad"), P("rad"), P("rad"), P("rad")),
        out_specs=(spec, spec),
        check_vma=False,
    )
```
